32 devices in a mesh: parts: 2 (over y), tensor: 4 (over x, core), dp: 4 (over z).
Axes of the slice: x: 2, y: 2, z: 4, core: 2. Of those that a mesh axis runs over, the one named last changes fastest.
Arguments:
- hidden: bfloat16 [2048, 53248], P(('parts', 'dp'), 'tensor'), parts along dimension 0, may hold values from -6 to 6
- down_weight: bfloat16 [53248, 512], P('tensor'), may hold values from -0.02734375 to 0.02734375
- cotangent: bfloat16 [2048, 512], P(('parts', 'dp')), parts along dimension 0, may hold values from -64 to 64
Outputs:
- output: bfloat16 [2048, 512], P(('parts', 'dp')), parts along dimension 0
- weight_grad: bfloat16 [106496, 512], P(('parts', 'tensor')), parts along dimension 0
- hidden_grad: bfloat16 [2048, 53248], P(('parts', 'dp'), 'tensor'), parts along dimension 0
The draws below stay inside these ranges and needn't reach their ends.
There are 2 independent parts, one for each index of `parts`. The reference program is written for one: setup_inputs(seed, part) draws one part's arguments, and reference() takes and returns one part's arrays. A program takes and returns all parts, laid end to end along the dimension named above; an argument that names none is the same for every part. Nothing has to cross between parts.
All inputs are finite; a program needn't handle non-finite values.
Results may differ from the reference program's by a relative error of at most 0.0051.
Values may be sent and summed in bfloat16 or wider, within the bound.
No kernel may reach another device: no remote copies, remote signals or barrier semaphores. Data moves between devices by JAX's collectives and lax.ppermute only.
A program may use at most 192 MiB of HBM per device.

```python
import math
import jax
import jax.numpy as jnp
from jax import lax

FF = 53248
HAD = 4096
GROUPS = 13
D_WIN = 512
TOKENS = 1024
N_TENSOR = 4


def shard_levels(rng, shape, pieces, low, high):
    def one(position, shards_of):
        draws = jax.random.uniform(jax.random.fold_in(jax.random.fold_in(rng, 6), position), (shards_of,), jnp.float32, low / len(pieces), high / len(pieces))
        return jnp.repeat(jnp.exp(draws), shape[position] // shards_of).reshape((-1,) + (1,) * (len(shape) - position - 1))

    loudness = one(*pieces[0])
    for cut in pieces[1:]:
        loudness = loudness * one(*cut)
    return loudness


def noise(own_key, dims, width, bound, cuts=(), kind=jnp.bfloat16):
    result = jax.random.normal(own_key, dims, jnp.float32) * width
    if len(cuts) > 0:
        result = shard_levels(own_key, dims, cuts, -0.22, 0.18) * result
    return jnp.clip(result, min=-bound, max=bound).astype(kind)


def setup_inputs(seed: int = 0, part: int = 0) -> dict:
    splits = jax.random.split(jax.random.key(seed), 4)
    part_keys = jax.random.split(jax.random.fold_in(splits[3], part), 4)
    return {
        "hidden": noise(part_keys[0], (TOKENS, FF), 1.0, 6.0, ((0, 4), (1, 4))),
        "down_weight": noise(splits[1], (FF, D_WIN), FF ** -0.5, 0.02734375, ((0, 4),)),
        "cotangent": noise(part_keys[2], (TOKENS, D_WIN), ((FF / D_WIN) ** 0.5), 64.0, ((0, 4),)),
    }


def sign_table(order_size):
    indices = jnp.arange(order_size, dtype=jnp.int32)
    intersection = jnp.bitwise_and(indices[:, None], indices[None, :])
    parity_count = jnp.zeros((order_size, order_size), jnp.int32)
    for bit_pos in range(order_size.bit_length() - 1):
        parity_count = parity_count + jnp.bitwise_and(jnp.right_shift(intersection, bit_pos), 1)
    return (1 - 2 * jnp.bitwise_and(parity_count, 1)).astype(jnp.float32)

def rotate(values):
    row_count = values.shape[0]
    local_size = HAD // N_TENSOR
    blocks = values.astype(jnp.float32).reshape(row_count, N_TENSOR, GROUPS, local_size)
    inner_sum = jnp.einsum('rpcq,qs->rpcs', blocks, sign_table(local_size), precision=lax.Precision.HIGHEST)
    outer_sum = jnp.einsum('rpcs,pt->rtcs', inner_sum, sign_table(N_TENSOR), precision=lax.Precision.HIGHEST)
    return (outer_sum / math.sqrt(HAD)).reshape(row_count, FF).astype(jnp.bfloat16)

def reference(hidden, down_weight, cotangent):
    rotated = rotate(hidden)
    output = jnp.dot(rotated, down_weight, preferred_element_type=jnp.float32).astype(jnp.bfloat16)
    weight_grad = (jnp.dot(rotated.T, cotangent, preferred_element_type=jnp.float32) / TOKENS).astype(jnp.bfloat16)
    back_grad = jnp.dot(cotangent, down_weight.T, preferred_element_type=jnp.float32).astype(jnp.bfloat16)
    hidden_grad = rotate(back_grad)
    return (output, weight_grad, hidden_grad)
```

```python
import math

import jax
import jax.numpy as jnp
from jax import lax
from jax.sharding import PartitionSpec as P

HAD = 4096
GROUPS = 13
CHUNKS = (1, 2, 2, 2, 2, 2, 2)
BF = jnp.bfloat16
F32 = jnp.float32


def sign_table(order_size, kind):
    indices = jnp.arange(order_size, dtype=jnp.int32)
    intersection = jnp.bitwise_and(indices[:, None], indices[None, :])
    parity_count = jnp.zeros((order_size, order_size), jnp.int32)
    for bit_pos in range(order_size.bit_length() - 1):
        parity_count = parity_count + jnp.bitwise_and(jnp.right_shift(intersection, bit_pos), 1)
    return (1 - 2 * jnp.bitwise_and(parity_count, 1)).astype(kind)


def across(values):
    size = lax.axis_size("tensor")
    position = lax.axis_index("tensor")
    current = values.astype(F32)
    for bit_pos in reversed(range(size.bit_length() - 1)):
        partner = lax.ppermute(
            current.astype(BF), "tensor", [(i, i ^ 1 << bit_pos) for i in range(size)]
        )
        sign = (1 - 2 * jnp.bitwise_and(jnp.right_shift(position, bit_pos), 1)).astype(F32)
        current = partner.astype(F32) + sign * current
    return current


def rotate(values, table):
    rows, width = values.shape
    size = table.shape[0]
    mixed = (across(values) * (1.0 / math.sqrt(HAD))).astype(BF)
    turned = jnp.einsum(
        "rcq,qs->rcs", mixed.reshape(rows, width // size, size), table,
        preferred_element_type=F32,
    )
    return turned.reshape(rows, width).astype(BF)


def grad_product(rows, cotangent):
    return lax.dot_general(rows, cotangent, (((0,), (0,)), ((), ())), preferred_element_type=F32)


def over_tokens(rotated, cotangent, outer_cotangent, scale):
    count = lax.axis_size("dp")
    place = lax.axis_index("dp")
    last, half = count - 1, count // 2
    partial = grad_product(rotated, cotangent)
    if half > 1:
        outer = lax.ppermute(rotated, "dp", [(0, 1), (last, last - 1)])
        partial = grad_product(
            jnp.concatenate([rotated, outer], 0),
            jnp.concatenate([cotangent, outer_cotangent], 0),
        )
    for step in range(1, half - 1):
        outer = lax.ppermute(
            partial.astype(BF), "dp", [(step, step + 1), (last - step, last - step - 1)]
        )
        partial = partial + outer.astype(F32)
    mine = partial.astype(BF)
    other = lax.ppermute(mine, "dp", [(half - 1, half), (half, half - 1)])
    total = ((mine.astype(F32) + other.astype(F32)) * scale).astype(BF)
    for step in range(half - 1, 0, -1):
        inner = lax.ppermute(total, "dp", [(step, step - 1), (last - step, last - step + 1)])
        total = jnp.where((place == step - 1) | (place == last - step + 1), inner, total)
    return total


def local(hidden, down_weight, cotangent):
    local_size = HAD // lax.axis_size("tensor")
    count = lax.axis_size("dp")
    table = sign_table(local_size, BF)
    scale = 1.0 / (cotangent.shape[0] * count)
    outer_cotangent = cotangent
    if count > 2:
        outer_cotangent = lax.ppermute(
            cotangent, "dp", [(0, 1), (count - 1, count - 2)]
        )
    grads, backs, part_out = [], [], None
    start = 0
    for groups in CHUNKS:
        span = slice(start * local_size, (start + groups) * local_size)
        start += groups
        rotated = rotate(hidden[:, span], table)
        grads.append(over_tokens(rotated, cotangent, outer_cotangent, scale))
        term = jnp.dot(rotated, down_weight[span], preferred_element_type=F32)
        part_out = term if part_out is None else part_out + term
        back = lax.dot_general(
            cotangent, down_weight[span], (((1,), (1,)), ((), ())), preferred_element_type=F32
        ).astype(BF)
        backs.append(rotate(back, table))
    output = lax.psum(part_out, "tensor").astype(BF)
    return (output, jnp.concatenate(grads, 0), jnp.concatenate(backs, 1))


def solution(mesh):
    return jax.shard_map(
        local,
        mesh=mesh,
        in_specs=(P(("parts", "dp"), "tensor"), P("tensor", None), P(("parts", "dp"), None)),
        out_specs=(
            P(("parts", "dp"), None),
            P(("parts", "tensor"), None),
            P(("parts", "dp"), "tensor"),
        ),
        check_vma=False,
    )
```

```python
import math

import jax
import jax.numpy as jnp
from jax import lax
from jax.experimental import pallas as pl
from jax.experimental.pallas import tpu as pltpu
from jax.sharding import PartitionSpec as P

HAD = 4096
GROUPS = 13
CHUNKS = (1, 1, 2, 2, 2, 2, 2, 1)
BF = jnp.bfloat16
F32 = jnp.float32
ANY = pl.BlockSpec(memory_space=pl.ANY)
SCALARS = pl.BlockSpec(memory_space=pltpu.SMEM)
VMEM_BYTES = 48 * 2**20


def sign_table(order_size, kind):
    indices = jnp.arange(order_size, dtype=jnp.int32)
    intersection = jnp.bitwise_and(indices[:, None], indices[None, :])
    parity_count = jnp.zeros((order_size, order_size), jnp.int32)
    for bit_pos in range(order_size.bit_length() - 1):
        parity_count = parity_count + jnp.bitwise_and(jnp.right_shift(intersection, bit_pos), 1)
    return (1 - 2 * jnp.bitwise_and(parity_count, 1)).astype(kind)


def combined(signs, values, partners):
    current = values.astype(F32)
    for stage, partner in enumerate(partners):
        current = partner.astype(F32) + signs[stage] * current
    return current


def turned(mixed, table):
    base = table.shape[0]
    count = mixed.shape[1] // base
    parts = [
        jnp.dot(mixed[:, i * base:(i + 1) * base], table, preferred_element_type=F32)
        for i in range(count)
    ]
    stride = 1
    while stride < count:
        parts = [
            parts[i] + parts[i ^ stride] if not i & stride else parts[i ^ stride] - parts[i]
            for i in range(count)
        ]
        stride *= 2
    return parts


class Chain:
    def __init__(self):
        self.token = None

    def __call__(self, body, groups, ins, outs, flops=0, aliases=None):
        arrays = [a for a, _ in ins]
        specs = [s for _, s in ins]
        count = len(arrays)
        if self.token is not None:
            arrays.append(self.token)
            specs.append(ANY)
        total = len(arrays)

        def kernel(*refs):
            body(*refs[:count], *refs[total:])

        size = sum(math.prod(s.shape) * s.dtype.itemsize for s, _ in outs)
        results = pl.pallas_call(
            kernel,
            grid=(groups,),
            in_specs=specs,
            out_specs=[s for _, s in outs],
            out_shape=[s for s, _ in outs],
            input_output_aliases=aliases or {},
            compiler_params=pltpu.CompilerParams(vmem_limit_bytes=VMEM_BYTES),
            cost_estimate=pl.CostEstimate(flops=flops, bytes_accessed=3 * size, transcendentals=0),
        )(*arrays)
        self.token = results[0]
        return results


def local(hidden, down_weight, cotangent):
    tensor_size, dp_size = lax.axis_size("tensor"), lax.axis_size("dp")
    position, place = lax.axis_index("tensor"), lax.axis_index("dp")
    last, half = dp_size - 1, dp_size // 2
    rows, width = hidden.shape
    features = cotangent.shape[1]
    unit = width // GROUPS
    table = sign_table(min(unit, 256), BF)
    scale = 1.0 / (rows * dp_size)
    root = 1.0 / math.sqrt(HAD)
    strides = [1 << b for b in reversed(range(tensor_size.bit_length() - 1))]
    stages = len(strides)
    signs = jnp.stack(
        [jnp.where(jnp.bitwise_and(position, s) != 0, -1.0, 1.0).astype(F32) for s in strides]
    )
    chain = Chain()
    starts = [sum(CHUNKS[:j]) for j in range(len(CHUNKS))]
    row_block = (rows, unit)
    grad_block = (unit, features)

    def column(first=0):
        return pl.BlockSpec(row_block, lambda g: (0, first + g))

    def grad_rows(first=0):
        return pl.BlockSpec(grad_block, lambda g: (first + g, 0))

    def whole(array):
        return pl.BlockSpec(array.shape, lambda g: (0,) * array.ndim)

    def strip(j):
        return jax.ShapeDtypeStruct((rows, CHUNKS[j] * unit), BF)

    def grad_shape(j):
        return jax.ShapeDtypeStruct((CHUNKS[j] * unit, features), BF)

    def swap(array, stage):
        stride = strides[stage]
        return lax.ppermute(array, "tensor", [(i, i ^ stride) for i in range(tensor_size)])

    def copied(values, first, j):
        def body(v_ref, o_ref):
            o_ref[...] = v_ref[...]
        return chain(body, CHUNKS[j], [(values, column(first))], [(strip(j), column())])[0]

    def mixed(values, first, partners, j):
        def body(s_ref, v_ref, *refs):
            refs[-1][...] = combined(s_ref, v_ref[...], [r[...] for r in refs[:-1]]).astype(BF)
        ins = [(signs, SCALARS), (values, column(first))] + [(p, column()) for p in partners]
        return chain(body, CHUNKS[j], ins, [(strip(j), column())])[0]

    def rotated_strip(values, first, partners, j, into=None):
        def body(s_ref, v_ref, t_ref, *refs):
            o_ref = refs[-1]
            mix = combined(s_ref, v_ref[...], [r[...] for r in refs[:stages]]) * root
            base = t_ref.shape[0]
            for i, part in enumerate(turned(mix.astype(BF), t_ref[...])):
                o_ref[:, i * base:(i + 1) * base] = part.astype(BF)
        ins = [(signs, SCALARS), (values, column(first)), (table, whole(table))]
        ins += [(p, column()) for p in partners]
        out, spec, aliases = strip(j), column(), None
        if into is not None:
            out, spec = jax.ShapeDtypeStruct((rows, width), BF), column(starts[j])
            if into[0] is not None:
                aliases = {len(ins): 0}
                ins.append((into[0], ANY))
        return chain(
            body, CHUNKS[j], ins, [(out, spec)],
            2 * rows * CHUNKS[j] * unit * table.shape[0], aliases,
        )[0]

    def partial_grad(own, outer, outer_cotangent, j):
        pairs = [(own, cotangent)] + ([(outer, outer_cotangent)] if outer is not None else [])
        def body(*refs):
            total = None
            for k in range(len(pairs)):
                term = lax.dot_general(
                    refs[2 * k][...], refs[2 * k + 1][...], (((0,), (0,)), ((), ())),
                    preferred_element_type=F32,
                )
                total = term if total is None else total + term
            refs[-1][...] = total.astype(BF)
        ins = []
        for r, c in pairs:
            ins += [(r, column()), (c, whole(c))]
        return chain(
            body, CHUNKS[j], ins, [(grad_shape(j), grad_rows())],
            2 * len(pairs) * rows * CHUNKS[j] * unit * features,
        )[0]

    def added(mine, other, factor, j):
        def body(a_ref, b_ref, o_ref):
            o_ref[...] = ((a_ref[...].astype(F32) + b_ref[...].astype(F32)) * factor).astype(BF)
        return chain(
            body, CHUNKS[j], [(mine, grad_rows()), (other, grad_rows())],
            [(grad_shape(j), grad_rows())],
        )[0]

    def placed(total, inners, flags, buffer, j):
        def body(f_ref, t_ref, *refs):
            value = t_ref[...]
            for k in range(len(inners)):
                value = jnp.where(f_ref[k] != 0, refs[k][...], value)
            refs[-1][...] = value
        ins = [(flags, SCALARS), (total, grad_rows())] + [(i, grad_rows()) for i in inners]
        aliases = None
        if buffer is not None:
            aliases = {len(ins): 0}
            ins.append((buffer, ANY))
        return chain(
            body, CHUNKS[j], ins,
            [(jax.ShapeDtypeStruct((width, features), BF), grad_rows(starts[j]))],
            0, aliases,
        )[0]

    def products(rotated, part_out, j):
        def body(c_ref, w_ref, r_ref, *refs):
            back_ref, out_ref = refs[-2:]
            back_ref[...] = lax.dot_general(
                c_ref[...], w_ref[...], (((1,), (1,)), ((), ())), preferred_element_type=F32
            ).astype(BF)

            @pl.when(pl.program_id(0) == 0)
            def _():
                out_ref[...] = refs[0][...] if part_out is not None else jnp.zeros_like(out_ref)

            out_ref[...] += jnp.dot(r_ref[...], w_ref[...], preferred_element_type=F32)
        ins = [(cotangent, whole(cotangent)), (down_weight, grad_rows(starts[j])), (rotated, column())]
        if part_out is not None:
            ins.append((part_out, whole(part_out)))
        shape = jax.ShapeDtypeStruct((rows, features), F32)
        return chain(
            body, CHUNKS[j], ins,
            [(strip(j), column()), (shape, pl.BlockSpec(shape.shape, lambda g: (0, 0)))],
            4 * rows * CHUNKS[j] * unit * features,
        )

    outer_cotangent = None
    if half > 1:
        outer_cotangent = lax.ppermute(cotangent, "dp", [(0, 1), (last, last - 1)])
    flags = jnp.stack([
        ((place == s - 1) | (place == last - s + 1)).astype(jnp.int32) for s in range(half - 1, 0, -1)
    ] or [jnp.int32(0)])

    n = len(CHUNKS)
    got = [[] for _ in range(n)]
    back_got = [[] for _ in range(n)]
    rotated, backs, outer, mine, other, total, inner = ([None] * n for _ in range(7))
    state = {"grad": None, "hidden_grad": None, "out": None}

    def send_hidden(j):
        got[j].append(swap(copied(hidden, starts[j], j), 0))

    def mix_hidden(j, stage):
        got[j].append(swap(mixed(hidden, starts[j], got[j], j), stage))

    def turn_hidden(j):
        rotated[j] = rotated_strip(hidden, starts[j], got[j], j)
        if half > 1:
            outer[j] = lax.ppermute(rotated[j], "dp", [(0, 1), (last, last - 1)])

    def send_partial(j):
        mine[j] = partial_grad(rotated[j], outer[j], outer_cotangent, j)
        for step in range(1, half - 1):
            came = lax.ppermute(mine[j], "dp", [(step, step + 1), (last - step, last - step - 1)])
            mine[j] = added(mine[j], came, 1.0, j)
        other[j] = lax.ppermute(mine[j], "dp", [(half - 1, half), (half, half - 1)])

    def send_total(j):
        total[j] = added(mine[j], other[j], scale, j)
        inner[j] = []
        moving = total[j]
        for step in range(half - 1, 0, -1):
            moving = lax.ppermute(moving, "dp", [(step, step - 1), (last - step, last - step + 1)])
            inner[j].append(moving)

    def place_grad(j):
        state["grad"] = placed(total[j], inner[j], flags, state["grad"], j)

    def send_back(j):
        backs[j], state["out"] = products(rotated[j], state["out"], j)
        back_got[j].append(swap(backs[j], 0))

    def mix_back(j, stage):
        back_got[j].append(swap(mixed(backs[j], 0, back_got[j], j), stage))

    def turn_back(j):
        state["hidden_grad"] = rotated_strip(backs[j], 0, back_got[j], j, (state["hidden_grad"],))

    def on(step, j, *args):
        if 0 <= j < n:
            step(j, *args)

    send_hidden(0)
    on(send_hidden, 1)
    for s in range(1, stages):
        mix_hidden(0, s)
    on(send_hidden, 2)
    turn_hidden(0)
    for s in range(1, stages):
        on(mix_hidden, 1, s)
    on(turn_hidden, 1)
    send_back(0)
    send_partial(0)
    for i in range(n + 1):
        on(send_hidden, i + 3)
        for s in range(1, stages):
            on(mix_hidden, i + 2, s)
            on(mix_back, i, s)
        on(send_back, i + 1)
        on(turn_hidden, i + 2)
        on(send_partial, i + 1)
        on(turn_back, i)
        on(send_total, i)
        on(place_grad, i - 1)
    output = state["out"]
    for stage in range(stages):
        output = output + swap(output, stage)
    return (output.astype(BF), state["grad"], state["hidden_grad"])


def solution(mesh):
    return jax.shard_map(
        local,
        mesh=mesh,
        in_specs=(P(("parts", "dp"), "tensor"), P("tensor", None), P(("parts", "dp"), None)),
        out_specs=(
            P(("parts", "dp"), None),
            P(("parts", "tensor"), None),
            P(("parts", "dp"), "tensor"),
        ),
        check_vma=False,
    )
```

```python
import math

import jax
import jax.numpy as jnp
from jax import lax
from jax.experimental import pallas as pl
from jax.experimental.pallas import tpu as pltpu
from jax.sharding import PartitionSpec as P

HAD = 4096
GROUPS = 13
CHUNKS = (1, 1, 2, 2, 2, 2, 2, 1)
LAG = 3
BF = jnp.bfloat16
F32 = jnp.float32
ANY = pl.BlockSpec(memory_space=pl.ANY)
SCALARS = pl.BlockSpec(memory_space=pltpu.SMEM)
VMEM_BYTES = 48 * 2**20


def sign_table(order_size, kind):
    indices = jnp.arange(order_size, dtype=jnp.int32)
    intersection = jnp.bitwise_and(indices[:, None], indices[None, :])
    parity_count = jnp.zeros((order_size, order_size), jnp.int32)
    for bit_pos in range(order_size.bit_length() - 1):
        parity_count = parity_count + jnp.bitwise_and(jnp.right_shift(intersection, bit_pos), 1)
    return (1 - 2 * jnp.bitwise_and(parity_count, 1)).astype(kind)


def turned(mixed, table):
    base = table.shape[0]
    count = mixed.shape[1] // base
    parts = [
        jnp.dot(mixed[:, i * base:(i + 1) * base], table, preferred_element_type=F32)
        for i in range(count)
    ]
    stride = 1
    while stride < count:
        parts = [
            parts[i] + parts[i ^ stride] if not i & stride else parts[i ^ stride] - parts[i]
            for i in range(count)
        ]
        stride *= 2
    return parts


class Chain:
    def __init__(self):
        self.token = None
        self.after = []

    def __call__(self, name, body, groups, ins, outs, aliases=None):
        arrays = [a for a, _ in ins]
        specs = [s for _, s in ins]
        count = len(arrays)
        for late in [self.token] + self.after:
            if late is not None and all(a is not late for a in arrays):
                arrays.append(late)
                specs.append(ANY)
        self.after = []
        total = len(arrays)

        def kernel(*refs):
            body(*refs[:count], *refs[total:])

        results = pl.pallas_call(
            kernel,
            grid=(groups,),
            name=name,
            in_specs=specs,
            out_specs=[s for _, s in outs],
            out_shape=[s for s, _ in outs],
            input_output_aliases=aliases or {},
            compiler_params=pltpu.CompilerParams(vmem_limit_bytes=VMEM_BYTES),
            cost_estimate=pl.CostEstimate(flops=1, bytes_accessed=1, transcendentals=0),
        )(*arrays)
        self.token = results[0]
        return results


def local(hidden, down_weight, cotangent):
    tensor_size, dp_size = lax.axis_size("tensor"), lax.axis_size("dp")
    position, place = lax.axis_index("tensor"), lax.axis_index("dp")
    last, half = dp_size - 1, dp_size // 2
    rows, width = hidden.shape
    features = cotangent.shape[1]
    unit = width // GROUPS
    table = sign_table(min(unit, 256), BF)
    scale = 1.0 / (rows * dp_size)
    root = 1.0 / math.sqrt(HAD)
    strides = [1 << b for b in reversed(range(tensor_size.bit_length() - 1))]
    stages = len(strides) - 1
    signs = jnp.stack(
        [jnp.where(jnp.bitwise_and(position, s) != 0, -1.0, 1.0).astype(F32) for s in strides]
    )
    chain = Chain()
    starts = [sum(CHUNKS[:j]) for j in range(len(CHUNKS))]
    row_block = (rows, unit)
    grad_block = (unit, features)

    def column(first=0):
        return pl.BlockSpec(row_block, lambda g: (0, first + g))

    def grad_rows(first=0):
        return pl.BlockSpec(grad_block, lambda g: (first + g, 0))

    def whole(array):
        return pl.BlockSpec(array.shape, lambda g: (0,) * array.ndim)

    def grad_shape(j):
        return jax.ShapeDtypeStruct((CHUNKS[j] * unit, features), BF)

    def swap(array, stage):
        stride = strides[stage]
        pairs = [(i, i ^ stride) for i in range(tensor_size)]
        if isinstance(array, (list, tuple)):
            return [lax.ppermute(a, "tensor", pairs) for a in array]
        return lax.ppermute(array, "tensor", pairs)

    def copied(j, size):
        def body(v_ref, o_ref):
            o_ref[...] = v_ref[...]
        shape = jax.ShapeDtypeStruct((rows, size * unit), BF)
        return chain(
            "copied", body, CHUNKS[j], [(hidden, column(starts[j]))], [(shape, column())]
        )[0]

    def across(refs, partners):
        current = refs[1][...].astype(F32)
        for stage in range(partners):
            current = refs[2 + stage][...].astype(F32) + refs[0][stage] * current
        return current

    def mixed(own, count, partners):
        def body(*refs):
            refs[-1][...] = across(refs, len(partners)).astype(BF)
        ins = [(signs, SCALARS)] + [(v, column(at)) for v, at in [own] + partners]
        shape = jax.ShapeDtypeStruct((rows, count * unit), BF)
        return chain("mixed", body, count, ins, [(shape, column())])[0]

    def rotated_strip(own, count, partners, into=None, at=0):
        def body(*refs):
            o_ref, t_ref = refs[-1], refs[table_at]
            base = t_ref.shape[0]
            mix = (across(refs, stages) * root).astype(BF)
            for i, part in enumerate(turned(mix, t_ref[...])):
                o_ref[:, i * base:(i + 1) * base] = part.astype(BF)
        ins = [(signs, SCALARS)] + [(v, column(first)) for v, first in [own] + partners]
        table_at = len(ins)
        ins.append((table, whole(table)))
        out = jax.ShapeDtypeStruct((rows, count * unit if into is None else width), BF)
        aliases = None
        if into is not None and into[0] is not None:
            aliases = {len(ins): 0}
            ins.append((into[0], ANY))
        return chain("rotated", body, count, ins, [(out, column(at))], aliases)[0]

    def partial_grad(own, outer, outer_cotangent, j):
        pairs = [(own, cotangent)] + ([(outer, outer_cotangent)] if outer is not None else [])
        def body(*refs):
            total = None
            for k in range(len(pairs)):
                term = lax.dot_general(
                    refs[2 * k][...], refs[2 * k + 1][...], (((0,), (0,)), ((), ())),
                    preferred_element_type=F32,
                )
                total = term if total is None else total + term
            refs[-1][...] = total.astype(BF)
        ins = []
        for r, c in pairs:
            ins += [(r, column()), (c, whole(c))]
        return chain(
            "partial_grad", body, CHUNKS[j], ins, [(grad_shape(j), grad_rows())],
        )[0]

    def added(mine, other, factor, j):
        def body(a_ref, b_ref, o_ref):
            o_ref[...] = ((a_ref[...].astype(F32) + b_ref[...].astype(F32)) * factor).astype(BF)
        return chain(
            "added", body, CHUNKS[j], [(mine, grad_rows()), (other, grad_rows())],
            [(grad_shape(j), grad_rows())],
        )[0]

    def chosen(total, inners, j):
        def body(f_ref, t_ref, *refs):
            value = t_ref[...]
            for k in range(len(inners)):
                value = jnp.where(f_ref[k] != 0, refs[k][...], value)
            refs[-1][...] = value
        ins = [(flags, SCALARS), (total, grad_rows())] + [(i, grad_rows()) for i in inners]
        return chain("chosen", body, CHUNKS[j], ins, [(grad_shape(j), grad_rows())])[0]

    def placed(mine, partner, buffer, j):
        def body(s_ref, a_ref, b_ref, *refs):
            value = b_ref[...].astype(F32) + s_ref[stages] * a_ref[...].astype(F32)
            refs[-1][...] = value.astype(BF)
        ins = [(signs, SCALARS), (mine, grad_rows()), (partner, grad_rows())]
        aliases = None
        if buffer is not None:
            aliases = {len(ins): 0}
            ins.append((buffer, ANY))
        return chain(
            "placed", body, CHUNKS[j], ins,
            [(jax.ShapeDtypeStruct((width, features), BF), grad_rows(starts[j]))],
            aliases,
        )[0]

    def products(rotated, part_out, buffer, first, size, j):
        def body(s_ref, c_ref, w_ref, p_ref, r_ref, *refs):
            back_ref, out_ref = refs[-2:]
            weights = (
                p_ref[...].astype(F32) + s_ref[stages] * w_ref[...].astype(F32)
            ).astype(BF)
            back_ref[...] = lax.dot_general(
                c_ref[...], weights, (((1,), (1,)), ((), ())), preferred_element_type=F32
            ).astype(BF)

            @pl.when(pl.program_id(0) == 0)
            def _():
                out_ref[...] = refs[0][...] if part_out is not None else jnp.zeros_like(out_ref)

            out_ref[...] += jnp.dot(r_ref[...], weights, preferred_element_type=F32)
        ins = [
            (signs, SCALARS), (cotangent, whole(cotangent)), (down_weight, grad_rows(starts[j])),
            (weight_partner, grad_rows(starts[j])), (rotated, column()),
        ]
        aliases = {}
        if part_out is not None:
            aliases[len(ins)] = 1
            ins.append((part_out, whole(part_out)))
        if buffer is not None:
            aliases[len(ins)] = 0
            ins.append((buffer, ANY))
        shape = jax.ShapeDtypeStruct((rows, features), F32)
        return chain(
            "products", body, CHUNKS[j], ins,
            [(jax.ShapeDtypeStruct((rows, size * unit), BF), column(first)),
             (shape, pl.BlockSpec(shape.shape, lambda g: (0, 0)))],
            aliases,
        )

    def joined(mine, other, kind):
        def body(a_ref, b_ref, o_ref):
            o_ref[...] = (a_ref[...] + b_ref[...]).astype(kind)
        return chain(
            "joined", body, 1, [(mine, whole(mine)), (other, whole(other))],
            [(jax.ShapeDtypeStruct(mine.shape, kind), whole(mine))],
        )[0]

    weight_partner = swap(down_weight, stages)
    outer_cotangent = None
    if half > 1:
        outer_cotangent = lax.ppermute(cotangent, "dp", [(0, 1), (last, last - 1)])
    flags = jnp.stack([
        ((place == s - 1) | (place == last - s + 1)).astype(jnp.int32) for s in range(half - 1, 0, -1)
    ] or [jnp.int32(0)])

    n = len(CHUNKS)
    sent = {}
    rotated, outer, mine, other, total, inner, whole_sum, partner_sum = (
        [None] * n for _ in range(8)
    )
    state = {"grad": None, "hidden_grad": None, "out": None}
    total_out = []

    def send(r):
        b = r - LAG
        ahead = CHUNKS[r] if r < n else 0
        size = ahead + (CHUNKS[b] if b >= 0 else 0)
        buffer = copied(r, size) if r < n else None
        if b >= 0:
            buffer, state["out"] = products(rotated[b], state["out"], buffer, ahead, size, b)
            if b == n - 1:
                total_out.append((state["out"], swap(state["out"], 0)))
        sent[r] = []
        came = swap(buffer, 0) if stages else None
        for own, groups, at in ((hidden, ahead, 0), (buffer, size - ahead, ahead)):
            first = starts[r] if own is hidden and groups else at
            sent[r].append(((own, first), groups, [(came, at)] if stages else []))

    def mix(r):
        for s in range(1, stages):
            for own, groups, came in sent[r]:
                if groups:
                    came.append((swap(mixed(own, groups, came), s), 0))

    def turn(r):
        own, groups, came = sent[r][0]
        rotated[r] = rotated_strip(own, groups, came)
        if half > 1:
            outer[r] = lax.ppermute(rotated[r], "dp", [(0, 1), (last, last - 1)])

    def turn_back(b):
        own, groups, came = sent[b + LAG][1]
        state["hidden_grad"] = rotated_strip(
            own, groups, came, (state["hidden_grad"],), starts[b]
        )

    def send_partial(j):
        mine[j] = partial_grad(rotated[j], outer[j], outer_cotangent, j)
        for step in range(1, half - 1):
            came = lax.ppermute(mine[j], "dp", [(step, step + 1), (last - step, last - step - 1)])
            mine[j] = added(mine[j], came, 1.0, j)
        other[j] = lax.ppermute(mine[j], "dp", [(half - 1, half), (half, half - 1)])

    def send_total(j):
        total[j] = added(mine[j], other[j], scale, j)
        inner[j] = []
        moving = total[j]
        for step in range(half - 1, 0, -1):
            moving = lax.ppermute(moving, "dp", [(step, step - 1), (last - step, last - step + 1)])
            inner[j].append(moving)

    def choose(j):
        whole_sum[j] = chosen(total[j], inner[j], j)
        partner_sum[j] = swap(whole_sum[j], stages)

    def place_grad(j):
        state["grad"] = placed(whole_sum[j], partner_sum[j], state["grad"], j)

    def on(step, j, end=n):
        if 0 <= j < end:
            step(j)

    send(0)
    send(1)
    mix(0)
    chain.after = [outer_cotangent]
    turn(0)
    send(2)
    mix(1)
    turn(1)
    send_partial(0)
    send(3)
    send_partial(1)
    mix(2)
    turn(2)
    send_total(0)
    def join(stage):
        mine, came = total_out[-1]
        output = joined(mine, came, F32 if stage < stages else BF)
        total_out.append((output, swap(output, stage + 1) if stage < stages else None))

    for r in range(3, n + LAG + 1):
        on(send, r + 1, n + LAG)
        on(send_partial, r - 1)
        if r == 3:
            choose(0)
        if r >= n:
            on(mix, r, n + LAG)
            on(turn_back, r - LAG)
        if r == n + LAG - 1:
            for stage in range(stages + 1):
                join(stage)
        on(send_total, r - 2)
        on(mix, r)
        on(turn, r)
        if r > 3:
            on(choose, r - 3)
        on(place_grad, r - 4)
        if r < n:
            turn_back(r - LAG)
    return (total_out[-1][0], state["grad"], state["hidden_grad"])


def solution(mesh):
    return jax.shard_map(
        local,
        mesh=mesh,
        in_specs=(P(("parts", "dp"), "tensor"), P("tensor", None), P(("parts", "dp"), None)),
        out_specs=(
            P(("parts", "dp"), None),
            P(("parts", "tensor"), None),
            P(("parts", "dp"), "tensor"),
        ),
        check_vma=False,
    )
```

```python
import math

import jax
import jax.numpy as jnp
from jax import lax
from jax.experimental import pallas as pl
from jax.experimental.pallas import tpu as pltpu
from jax.sharding import PartitionSpec as P

HAD = 4096
GROUPS = 13
CHUNKS = (1, 1, 2, 2, 2, 2, 2, 1)
LAG = 3
BF = jnp.bfloat16
F32 = jnp.float32
ANY = pl.BlockSpec(memory_space=pl.ANY)
SCALARS = pl.BlockSpec(memory_space=pltpu.SMEM)
VMEM_BYTES = 48 * 2**20


def sign_table(order_size, kind):
    indices = jnp.arange(order_size, dtype=jnp.int32)
    intersection = jnp.bitwise_and(indices[:, None], indices[None, :])
    parity_count = jnp.zeros((order_size, order_size), jnp.int32)
    for bit_pos in range(order_size.bit_length() - 1):
        parity_count = parity_count + jnp.bitwise_and(jnp.right_shift(intersection, bit_pos), 1)
    return (1 - 2 * jnp.bitwise_and(parity_count, 1)).astype(kind)


def turned(mixed, table):
    base = table.shape[0]
    count = mixed.shape[1] // base
    parts = [
        jnp.dot(mixed[:, i * base:(i + 1) * base], table, preferred_element_type=F32)
        for i in range(count)
    ]
    stride = 1
    while stride < count:
        parts = [
            parts[i] + parts[i ^ stride] if not i & stride else parts[i ^ stride] - parts[i]
            for i in range(count)
        ]
        stride *= 2
    return parts


class Chain:
    def __init__(self):
        self.token = None
        self.after = []

    def __call__(self, name, body, groups, ins, outs, aliases=None):
        arrays = [a for a, _ in ins]
        specs = [s for _, s in ins]
        count = len(arrays)
        for late in [self.token] + self.after:
            if late is not None and all(a is not late for a in arrays):
                arrays.append(late)
                specs.append(ANY)
        self.after = []
        total = len(arrays)

        def kernel(*refs):
            body(*refs[:count], *refs[total:])

        results = pl.pallas_call(
            kernel,
            grid=(groups,),
            name=name,
            in_specs=specs,
            out_specs=[s for _, s in outs],
            out_shape=[s for s, _ in outs],
            input_output_aliases=aliases or {},
            compiler_params=pltpu.CompilerParams(vmem_limit_bytes=VMEM_BYTES),
            cost_estimate=pl.CostEstimate(flops=1, bytes_accessed=1, transcendentals=0),
        )(*arrays)
        self.token = results[0]
        return results


def local(hidden, down_weight, cotangent):
    tensor_size, dp_size = lax.axis_size("tensor"), lax.axis_size("dp")
    position, place = lax.axis_index("tensor"), lax.axis_index("dp")
    last, half = dp_size - 1, dp_size // 2
    rows, width = hidden.shape
    features = cotangent.shape[1]
    unit = width // GROUPS
    table = sign_table(min(unit, 256), BF)
    scale = 1.0 / (rows * dp_size)
    root = 1.0 / math.sqrt(HAD)
    strides = [1 << b for b in reversed(range(tensor_size.bit_length() - 1))]
    stages = len(strides) - 1
    signs = jnp.stack(
        [jnp.where(jnp.bitwise_and(position, s) != 0, -1.0, 1.0).astype(F32) for s in strides]
    )
    chain = Chain()
    starts = [sum(CHUNKS[:j]) for j in range(len(CHUNKS))]
    row_block = (rows, unit)
    grad_block = (unit, features)

    def column(first=0):
        return pl.BlockSpec(row_block, lambda g: (0, first + g))

    def grad_rows(first=0):
        return pl.BlockSpec(grad_block, lambda g: (first + g, 0))

    def whole(array):
        return pl.BlockSpec(array.shape, lambda g: (0,) * array.ndim)

    def grad_shape(j):
        return jax.ShapeDtypeStruct((CHUNKS[j] * unit, features), BF)

    def swap(array, stage):
        stride = strides[stage]
        pairs = [(i, i ^ stride) for i in range(tensor_size)]
        if isinstance(array, (list, tuple)):
            return [lax.ppermute(a, "tensor", pairs) for a in array]
        return lax.ppermute(array, "tensor", pairs)

    def copied(j, size):
        def body(v_ref, o_ref):
            o_ref[...] = v_ref[...]
        shape = jax.ShapeDtypeStruct((rows, size * unit), BF)
        return chain(
            "copied", body, CHUNKS[j], [(hidden, column(starts[j]))], [(shape, column())]
        )[0]

    def across(refs, partners):
        current = refs[1][...].astype(F32)
        for stage in range(partners):
            current = refs[2 + stage][...].astype(F32) + refs[0][stage] * current
        return current

    def mixed(own, count, partners):
        def body(*refs):
            refs[-1][...] = across(refs, len(partners)).astype(BF)
        ins = [(signs, SCALARS)] + [(v, column(at)) for v, at in [own] + partners]
        shape = jax.ShapeDtypeStruct((rows, count * unit), BF)
        return chain("mixed", body, count, ins, [(shape, column())])[0]

    def rotated_strip(own, count, partners, into=None, at=0):
        def body(*refs):
            o_ref, t_ref = refs[-1], refs[table_at]
            base = t_ref.shape[0]
            mix = (across(refs, stages) * root).astype(BF)
            for i, part in enumerate(turned(mix, t_ref[...])):
                o_ref[:, i * base:(i + 1) * base] = part.astype(BF)
        ins = [(signs, SCALARS)] + [(v, column(first)) for v, first in [own] + partners]
        table_at = len(ins)
        ins.append((table, whole(table)))
        out = jax.ShapeDtypeStruct((rows, count * unit if into is None else width), BF)
        aliases = None
        if into is not None and into[0] is not None:
            aliases = {len(ins): 0}
            ins.append((into[0], ANY))
        return chain("rotated", body, count, ins, [(out, column(at))], aliases)[0]

    def partial_grad(own, outer, outer_cotangent, j):
        pairs = [(own, cotangent)] + ([(outer, outer_cotangent)] if outer is not None else [])
        def body(*refs):
            total = None
            for k in range(len(pairs)):
                term = lax.dot_general(
                    refs[2 * k][...], refs[2 * k + 1][...], (((0,), (0,)), ((), ())),
                    preferred_element_type=F32,
                )
                total = term if total is None else total + term
            refs[-1][...] = total.astype(BF)
        ins = []
        for r, c in pairs:
            ins += [(r, column()), (c, whole(c))]
        return chain(
            "partial_grad", body, CHUNKS[j], ins, [(grad_shape(j), grad_rows())],
        )[0]

    def added(mine, other, factor, j):
        def body(a_ref, b_ref, o_ref):
            o_ref[...] = ((a_ref[...].astype(F32) + b_ref[...].astype(F32)) * factor).astype(BF)
        return chain(
            "added", body, CHUNKS[j], [(mine, grad_rows()), (other, grad_rows())],
            [(grad_shape(j), grad_rows())],
        )[0]

    def chosen(total, inners, j):
        def body(f_ref, t_ref, *refs):
            value = t_ref[...]
            for k in range(len(inners)):
                value = jnp.where(f_ref[k] != 0, refs[k][...], value)
            refs[-1][...] = value
        ins = [(flags, SCALARS), (total, grad_rows())] + [(i, grad_rows()) for i in inners]
        return chain("chosen", body, CHUNKS[j], ins, [(grad_shape(j), grad_rows())])[0]

    def placed(mine, partner, buffer, j):
        def body(s_ref, a_ref, b_ref, *refs):
            value = b_ref[...].astype(F32) + s_ref[stages] * a_ref[...].astype(F32)
            refs[-1][...] = value.astype(BF)
        ins = [(signs, SCALARS), (mine, grad_rows()), (partner, grad_rows())]
        aliases = None
        if buffer is not None:
            aliases = {len(ins): 0}
            ins.append((buffer, ANY))
        return chain(
            "placed", body, CHUNKS[j], ins,
            [(jax.ShapeDtypeStruct((width, features), BF), grad_rows(starts[j]))],
            aliases,
        )[0]

    def products(rotated, part_out, buffer, first, size, j):
        def body(s_ref, c_ref, w_ref, p_ref, r_ref, *refs):
            back_ref, out_ref = refs[-2:]
            weights = (
                p_ref[...].astype(F32) + s_ref[stages] * w_ref[...].astype(F32)
            ).astype(BF)
            back_ref[...] = lax.dot_general(
                c_ref[...], weights, (((1,), (1,)), ((), ())), preferred_element_type=F32
            ).astype(BF)

            @pl.when(pl.program_id(0) == 0)
            def _():
                out_ref[...] = refs[0][...] if part_out is not None else jnp.zeros_like(out_ref)

            out_ref[...] += jnp.dot(r_ref[...], weights, preferred_element_type=F32)
        ins = [
            (signs, SCALARS), (cotangent, whole(cotangent)), (down_weight, grad_rows(starts[j])),
            (weight_partner, grad_rows(starts[j])), (rotated, column()),
        ]
        aliases = {}
        if part_out is not None:
            aliases[len(ins)] = 1
            ins.append((part_out, whole(part_out)))
        if buffer is not None:
            aliases[len(ins)] = 0
            ins.append((buffer, ANY))
        shape = jax.ShapeDtypeStruct((rows, features), F32)
        return chain(
            "products", body, CHUNKS[j], ins,
            [(jax.ShapeDtypeStruct((rows, size * unit), BF), column(first)),
             (shape, pl.BlockSpec(shape.shape, lambda g: (0, 0)))],
            aliases,
        )

    def joined(mine, other, kind):
        def body(a_ref, b_ref, o_ref):
            o_ref[...] = (a_ref[...] + b_ref[...]).astype(kind)
        return chain(
            "joined", body, 1, [(mine, whole(mine)), (other, whole(other))],
            [(jax.ShapeDtypeStruct(mine.shape, kind), whole(mine))],
        )[0]

    weight_partner = swap(down_weight, stages)
    outer_cotangent = None
    if half > 1:
        outer_cotangent = lax.ppermute(cotangent, "dp", [(0, 1), (last, last - 1)])
    flags = jnp.stack([
        ((place == s - 1) | (place == last - s + 1)).astype(jnp.int32) for s in range(half - 1, 0, -1)
    ] or [jnp.int32(0)])

    n = len(CHUNKS)
    sent = {}
    rotated, outer, mine, other, total, inner, whole_sum, partner_sum = (
        [None] * n for _ in range(8)
    )
    state = {"grad": None, "hidden_grad": None, "out": None}
    total_out = []

    def send(r):
        b = r - LAG
        ahead = CHUNKS[r] if r < n else 0
        size = ahead + (CHUNKS[b] if b >= 0 else 0)
        buffer = copied(r, size) if r < n else None
        if b >= 0:
            buffer, state["out"] = products(rotated[b], state["out"], buffer, ahead, size, b)
            if b == n - 1:
                total_out.append((state["out"], swap(state["out"], 0)))
        sent[r] = []
        came = swap(buffer, 0) if stages else None
        for own, groups, at in ((hidden, ahead, 0), (buffer, size - ahead, ahead)):
            first = starts[r] if own is hidden and groups else at
            sent[r].append(((own, first), groups, [(came, at)] if stages else []))

    def mix(r):
        for s in range(1, stages):
            for own, groups, came in sent[r]:
                if groups:
                    came.append((swap(mixed(own, groups, came), s), 0))

    def turn(r):
        own, groups, came = sent[r][0]
        rotated[r] = rotated_strip(own, groups, came)
        if half > 1:
            outer[r] = lax.ppermute(rotated[r], "dp", [(0, 1), (last, last - 1)])

    def turn_back(b):
        own, groups, came = sent[b + LAG][1]
        state["hidden_grad"] = rotated_strip(
            own, groups, came, (state["hidden_grad"],), starts[b]
        )

    def send_partial(j):
        mine[j] = partial_grad(rotated[j], outer[j], outer_cotangent, j)
        for step in range(1, half - 1):
            came = lax.ppermute(mine[j], "dp", [(step, step + 1), (last - step, last - step - 1)])
            mine[j] = added(mine[j], came, 1.0, j)
        other[j] = lax.ppermute(mine[j], "dp", [(half - 1, half), (half, half - 1)])

    def send_total(j):
        total[j] = added(mine[j], other[j], scale, j)
        inner[j] = []
        moving = total[j]
        for step in range(half - 1, 0, -1):
            moving = lax.ppermute(moving, "dp", [(step, step - 1), (last - step, last - step + 1)])
            inner[j].append(moving)

    def choose(j):
        whole_sum[j] = chosen(total[j], inner[j], j)
        partner_sum[j] = swap(whole_sum[j], stages)

    def place_grad(j):
        state["grad"] = placed(whole_sum[j], partner_sum[j], state["grad"], j)

    def on(step, j, end=n):
        if 0 <= j < end:
            step(j)

    send(0)
    send(1)
    mix(0)
    chain.after = [outer_cotangent]
    turn(0)
    send(2)
    mix(1)
    turn(1)
    send_partial(0)
    send_partial(1)
    send(3)
    mix(2)
    turn(2)
    send_total(0)
    def join(stage):
        mine, came = total_out[-1]
        output = joined(mine, came, F32 if stage < stages else BF)
        total_out.append((output, swap(output, stage + 1) if stage < stages else None))

    for r in range(3, n + LAG + 1):
        on(send, r + 1, n + LAG)
        on(send_partial, r - 1)
        if r < 5:
            choose(r - 3)
        if r >= n:
            on(mix, r, n + LAG)
            on(turn_back, r - LAG)
        if r == n + LAG - 1:
            for stage in range(stages + 1):
                join(stage)
        on(send_total, r - 2)
        on(mix, r)
        on(turn, r)
        if r > 4:
            on(choose, r - 3)
        on(place_grad, r - 4)
        if r < n:
            turn_back(r - LAG)
    return (total_out[-1][0], state["grad"], state["hidden_grad"])


def solution(mesh):
    return jax.shard_map(
        local,
        mesh=mesh,
        in_specs=(P(("parts", "dp"), "tensor"), P("tensor", None), P(("parts", "dp"), None)),
        out_specs=(
            P(("parts", "dp"), None),
            P(("parts", "tensor"), None),
            P(("parts", "dp"), "tensor"),
        ),
        check_vma=False,
    )
```

```python
import math

import jax
import jax.numpy as jnp
from jax import lax
from jax.experimental import pallas as pl
from jax.experimental.pallas import tpu as pltpu
from jax.sharding import PartitionSpec as P

HAD = 4096
GROUPS = 13
CHUNKS = (1, 1, 2, 2, 2, 2, 2, 1)
LAG = 3
BF = jnp.bfloat16
F32 = jnp.float32
ANY = pl.BlockSpec(memory_space=pl.ANY)
SCALARS = pl.BlockSpec(memory_space=pltpu.SMEM)
VMEM_BYTES = 48 * 2**20


def sign_table(order_size, kind):
    indices = jnp.arange(order_size, dtype=jnp.int32)
    intersection = jnp.bitwise_and(indices[:, None], indices[None, :])
    parity_count = jnp.zeros((order_size, order_size), jnp.int32)
    for bit_pos in range(order_size.bit_length() - 1):
        parity_count = parity_count + jnp.bitwise_and(jnp.right_shift(intersection, bit_pos), 1)
    return (1 - 2 * jnp.bitwise_and(parity_count, 1)).astype(kind)


def turned(mixed, table):
    base = table.shape[0]
    count = mixed.shape[1] // base
    parts = [
        jnp.dot(mixed[:, i * base:(i + 1) * base], table, preferred_element_type=F32)
        for i in range(count)
    ]
    stride = 1
    while stride < count:
        parts = [
            parts[i] + parts[i ^ stride] if not i & stride else parts[i ^ stride] - parts[i]
            for i in range(count)
        ]
        stride *= 2
    return parts


class Chain:
    def __init__(self):
        self.token = None
        self.after = []

    def __call__(self, name, body, groups, ins, outs, aliases=None):
        arrays = [a for a, _ in ins]
        specs = [s for _, s in ins]
        count = len(arrays)
        for late in [self.token] + self.after:
            if late is not None and all(a is not late for a in arrays):
                arrays.append(late)
                specs.append(ANY)
        self.after = []
        total = len(arrays)

        def kernel(*refs):
            body(*refs[:count], *refs[total:])

        results = pl.pallas_call(
            kernel,
            grid=(groups,),
            name=name,
            in_specs=specs,
            out_specs=[s for _, s in outs],
            out_shape=[s for s, _ in outs],
            input_output_aliases=aliases or {},
            compiler_params=pltpu.CompilerParams(vmem_limit_bytes=VMEM_BYTES),
            cost_estimate=pl.CostEstimate(flops=1, bytes_accessed=1, transcendentals=0),
        )(*arrays)
        self.token = results[0]
        return results


def local(hidden, down_weight, cotangent):
    tensor_size, dp_size = lax.axis_size("tensor"), lax.axis_size("dp")
    position, place = lax.axis_index("tensor"), lax.axis_index("dp")
    last, half = dp_size - 1, dp_size // 2
    rows, width = hidden.shape
    features = cotangent.shape[1]
    unit = width // GROUPS
    table = sign_table(min(unit, 256), BF)
    scale = 1.0 / (rows * dp_size)
    root = 1.0 / math.sqrt(HAD)
    strides = [1 << b for b in reversed(range(tensor_size.bit_length() - 1))]
    stages = len(strides) - 1
    signs = jnp.stack(
        [jnp.where(jnp.bitwise_and(position, s) != 0, -1.0, 1.0).astype(F32) for s in strides]
    )
    chain = Chain()
    starts = [sum(CHUNKS[:j]) for j in range(len(CHUNKS))]
    row_block = (rows, unit)
    grad_block = (unit, features)

    def column(first=0):
        return pl.BlockSpec(row_block, lambda g: (0, first + g))

    def grad_rows(first=0):
        return pl.BlockSpec(grad_block, lambda g: (first + g, 0))

    def grad_halves():
        return pl.BlockSpec((unit // 2, features), lambda g: (g, 0))

    def whole(array):
        return pl.BlockSpec(array.shape, lambda g: (0,) * array.ndim)

    def grad_shape(j):
        return jax.ShapeDtypeStruct((CHUNKS[j] * unit, features), BF)

    def swap(array, stage):
        stride = strides[stage]
        pairs = [(i, i ^ stride) for i in range(tensor_size)]
        if isinstance(array, (list, tuple)):
            return [lax.ppermute(a, "tensor", pairs) for a in array]
        return lax.ppermute(array, "tensor", pairs)

    def copied(j, size):
        def body(v_ref, o_ref):
            o_ref[...] = v_ref[...]
        shape = jax.ShapeDtypeStruct((rows, size * unit), BF)
        return chain(
            "copied", body, CHUNKS[j], [(hidden, column(starts[j]))], [(shape, column())]
        )[0]

    def across(refs, partners):
        current = refs[1][...].astype(F32)
        for stage in range(partners):
            current = refs[2 + stage][...].astype(F32) + refs[0][stage] * current
        return current

    def mixed(own, count, partners):
        def body(*refs):
            refs[-1][...] = across(refs, len(partners)).astype(BF)
        ins = [(signs, SCALARS)] + [(v, column(at)) for v, at in [own] + partners]
        shape = jax.ShapeDtypeStruct((rows, count * unit), BF)
        return chain("mixed", body, count, ins, [(shape, column())])[0]

    def rotated_strip(own, count, partners, into=None, at=0):
        def body(*refs):
            o_ref, t_ref = refs[-1], refs[table_at]
            base = t_ref.shape[0]
            mix = (across(refs, stages) * root).astype(BF)
            for i, part in enumerate(turned(mix, t_ref[...])):
                o_ref[:, i * base:(i + 1) * base] = part.astype(BF)
        ins = [(signs, SCALARS)] + [(v, column(first)) for v, first in [own] + partners]
        table_at = len(ins)
        ins.append((table, whole(table)))
        out = jax.ShapeDtypeStruct((rows, count * unit if into is None else width), BF)
        aliases = None
        if into is not None and into[0] is not None:
            aliases = {len(ins): 0}
            ins.append((into[0], ANY))
        return chain("rotated", body, count, ins, [(out, column(at))], aliases)[0]

    def partial_grad(own, outer, outer_cotangent, j):
        pairs = [(own, cotangent)] + ([(outer, outer_cotangent)] if outer is not None else [])
        def body(*refs):
            total = None
            for k in range(len(pairs)):
                term = lax.dot_general(
                    refs[2 * k][...], refs[2 * k + 1][...], (((0,), (0,)), ((), ())),
                    preferred_element_type=F32,
                )
                total = term if total is None else total + term
            refs[-1][...] = total.astype(BF)
        ins = []
        for r, c in pairs:
            ins += [(r, column()), (c, whole(c))]
        return chain(
            "partial_grad", body, CHUNKS[j], ins, [(grad_shape(j), grad_rows())],
        )[0]

    def added(mine, other, factor, j):
        def body(a_ref, b_ref, o_ref):
            o_ref[...] = ((a_ref[...].astype(F32) + b_ref[...].astype(F32)) * factor).astype(BF)
        return chain(
            "added", body, 2 * CHUNKS[j], [(mine, grad_halves()), (other, grad_halves())],
            [(grad_shape(j), grad_halves())],
        )[0]

    def chosen(total, inners, j):
        def body(f_ref, t_ref, *refs):
            value = t_ref[...]
            for k in range(len(inners)):
                value = jnp.where(f_ref[k] != 0, refs[k][...], value)
            refs[-1][...] = value
        ins = [(flags, SCALARS), (total, grad_rows())] + [(i, grad_rows()) for i in inners]
        return chain("chosen", body, CHUNKS[j], ins, [(grad_shape(j), grad_rows())])[0]

    def placed(mine, partner, buffer, j):
        def body(s_ref, a_ref, b_ref, *refs):
            value = b_ref[...].astype(F32) + s_ref[stages] * a_ref[...].astype(F32)
            refs[-1][...] = value.astype(BF)
        ins = [(signs, SCALARS), (mine, grad_rows()), (partner, grad_rows())]
        aliases = None
        if buffer is not None:
            aliases = {len(ins): 0}
            ins.append((buffer, ANY))
        return chain(
            "placed", body, CHUNKS[j], ins,
            [(jax.ShapeDtypeStruct((width, features), BF), grad_rows(starts[j]))],
            aliases,
        )[0]

    def products(rotated, part_out, buffer, first, size, j):
        def body(s_ref, c_ref, w_ref, p_ref, r_ref, *refs):
            back_ref, out_ref = refs[-2:]
            weights = (
                p_ref[...].astype(F32) + s_ref[stages] * w_ref[...].astype(F32)
            ).astype(BF)
            back_ref[...] = lax.dot_general(
                c_ref[...], weights, (((1,), (1,)), ((), ())), preferred_element_type=F32
            ).astype(BF)

            @pl.when(pl.program_id(0) == 0)
            def _():
                out_ref[...] = refs[0][...] if part_out is not None else jnp.zeros_like(out_ref)

            out_ref[...] += jnp.dot(r_ref[...], weights, preferred_element_type=F32)
        ins = [
            (signs, SCALARS), (cotangent, whole(cotangent)), (down_weight, grad_rows(starts[j])),
            (weight_partner, grad_rows(starts[j])), (rotated, column()),
        ]
        aliases = {}
        if part_out is not None:
            aliases[len(ins)] = 1
            ins.append((part_out, whole(part_out)))
        if buffer is not None:
            aliases[len(ins)] = 0
            ins.append((buffer, ANY))
        shape = jax.ShapeDtypeStruct((rows, features), F32)
        return chain(
            "products", body, CHUNKS[j], ins,
            [(jax.ShapeDtypeStruct((rows, size * unit), BF), column(first)),
             (shape, pl.BlockSpec(shape.shape, lambda g: (0, 0)))],
            aliases,
        )

    def joined(mine, other, kind):
        def body(a_ref, b_ref, o_ref):
            o_ref[...] = (a_ref[...] + b_ref[...]).astype(kind)
        return chain(
            "joined", body, 1, [(mine, whole(mine)), (other, whole(other))],
            [(jax.ShapeDtypeStruct(mine.shape, kind), whole(mine))],
        )[0]

    weight_partner = swap(down_weight, stages)
    outer_cotangent = None
    if half > 1:
        outer_cotangent = lax.ppermute(cotangent, "dp", [(0, 1), (last, last - 1)])
    flags = jnp.stack([
        ((place == s - 1) | (place == last - s + 1)).astype(jnp.int32) for s in range(half - 1, 0, -1)
    ] or [jnp.int32(0)])

    n = len(CHUNKS)
    sent = {}
    rotated, outer, mine, other, total, inner, whole_sum, partner_sum = (
        [None] * n for _ in range(8)
    )
    state = {"grad": None, "hidden_grad": None, "out": None}
    total_out = []

    def send(r):
        b = r - LAG
        ahead = CHUNKS[r] if r < n else 0
        size = ahead + (CHUNKS[b] if b >= 0 else 0)
        buffer = copied(r, size) if r < n else None
        if b >= 0:
            buffer, state["out"] = products(rotated[b], state["out"], buffer, ahead, size, b)
            if b == n - 1:
                total_out.append((state["out"], swap(state["out"], 0)))
        sent[r] = []
        came = swap(buffer, 0) if stages else None
        for own, groups, at in ((hidden, ahead, 0), (buffer, size - ahead, ahead)):
            first = starts[r] if own is hidden and groups else at
            sent[r].append(((own, first), groups, [(came, at)] if stages else []))

    def mix(r):
        for s in range(1, stages):
            for own, groups, came in sent[r]:
                if groups:
                    came.append((swap(mixed(own, groups, came), s), 0))

    def turn(r):
        own, groups, came = sent[r][0]
        rotated[r] = rotated_strip(own, groups, came)
        if half > 1:
            outer[r] = lax.ppermute(rotated[r], "dp", [(0, 1), (last, last - 1)])

    def turn_back(b):
        own, groups, came = sent[b + LAG][1]
        state["hidden_grad"] = rotated_strip(
            own, groups, came, (state["hidden_grad"],), starts[b]
        )

    def send_partial(j):
        mine[j] = partial_grad(rotated[j], outer[j], outer_cotangent, j)
        for step in range(1, half - 1):
            came = lax.ppermute(mine[j], "dp", [(step, step + 1), (last - step, last - step - 1)])
            mine[j] = added(mine[j], came, 1.0, j)
        other[j] = lax.ppermute(mine[j], "dp", [(half - 1, half), (half, half - 1)])

    def send_total(j):
        total[j] = added(mine[j], other[j], scale, j)
        inner[j] = []
        moving = total[j]
        for step in range(half - 1, 0, -1):
            moving = lax.ppermute(moving, "dp", [(step, step - 1), (last - step, last - step + 1)])
            inner[j].append(moving)

    def choose(j):
        whole_sum[j] = chosen(total[j], inner[j], j)
        partner_sum[j] = swap(whole_sum[j], stages)

    def place_grad(j):
        state["grad"] = placed(whole_sum[j], partner_sum[j], state["grad"], j)

    def on(step, j, end=n):
        if 0 <= j < end:
            step(j)

    send(0)
    send(1)
    mix(0)
    chain.after = [outer_cotangent]
    turn(0)
    send(2)
    mix(1)
    turn(1)
    send_partial(0)
    send_partial(1)
    send(3)
    mix(2)
    turn(2)
    send_total(0)
    def join(stage):
        mine, came = total_out[-1]
        output = joined(mine, came, F32 if stage < stages else BF)
        total_out.append((output, swap(output, stage + 1) if stage < stages else None))

    for r in range(3, n + LAG + 1):
        on(send, r + 1, n + LAG)
        on(send_partial, r - 1)
        if r < 5:
            choose(r - 3)
        if r >= n:
            on(mix, r, n + LAG)
            on(turn_back, r - LAG)
        if r == n + LAG - 1:
            for stage in range(stages + 1):
                join(stage)
        on(send_total, r - 2)
        on(mix, r)
        on(turn, r)
        if r > 4:
            on(choose, r - 3)
        on(place_grad, r - 4)
        if r < n:
            turn_back(r - LAG)
    return (total_out[-1][0], state["grad"], state["hidden_grad"])


def solution(mesh):
    return jax.shard_map(
        local,
        mesh=mesh,
        in_specs=(P(("parts", "dp"), "tensor"), P("tensor", None), P(("parts", "dp"), None)),
        out_specs=(
            P(("parts", "dp"), None),
            P(("parts", "tensor"), None),
            P(("parts", "dp"), "tensor"),
        ),
        check_vma=False,
    )
```
